32 devices in a mesh: vir: 8 (over z, x), occ: 4 (over y, core).
Axes of the slice: x: 2, y: 2, z: 4, core: 2. Of those that a mesh axis runs over, the one named last changes fastest.
Arguments:
- integrals: bfloat16 [1024, 1024], P(None, 'vir'), as said below
- amplitudes: bfloat16 [1024, 256], P('vir', 'occ'), may hold values from -6 to 6
- labels: int32 [8], replicated, may hold values from 0 to 7
Outputs:
- residual: bfloat16 [1024, 256], P('vir', 'occ')
The draws below stay inside these ranges and needn't reach their ends.
Inputs may be any that keep to these rules, and one draw needn't show every extreme that they name: integrals is symmetric: integrals[x, y] == integrals[y, x].
All inputs are finite; a program needn't handle non-finite values.
Results may differ from the reference program's by a relative error of at most 0.001.
Values may be sent and summed in bfloat16 or wider, within the bound.
A program may use at most 64 MiB of HBM per device.

```python
import math
import jax
import jax.numpy as jnp
import numpy as np
from jax import lax

TILE = 128
NOCC = 16
OP = 256
NT = 8
PAIRS = 1024


def draw_integrals(key, part):
    base = jax.random.normal(key, (PAIRS, PAIRS), jnp.float32)
    spread = (4.0 / PAIRS) ** 0.5 * 0.70710678
    return ((base + base.T) * spread).astype(jnp.bfloat16)


def set_ends(entries, stream_key, low, largest):
    longest = entries.shape.index(max(entries.shape))
    spots = []
    for shift in (0, 1):
        where = [jax.random.randint(jax.random.fold_in(stream_key, axis), (), 0, length) for axis, length in enumerate(entries.shape)]
        where[longest] = (where[longest] + shift) % entries.shape[longest]
        spots.append(tuple(where))
    return entries.at[spots[0]].set(low).at[spots[1]].set(largest)


def shard_levels(rng, shape, cuts, smallest, top_value):
    gain = 1.0
    for axis_at, blocks in cuts:
        steps = jax.random.uniform(jax.random.fold_in(jax.random.fold_in(rng, 6), axis_at), (blocks,), jnp.float32, smallest / len(cuts), top_value / len(cuts))
        gain = gain * jnp.repeat(jnp.exp(steps), shape[axis_at] // blocks).reshape((-1,) + (1,) * (len(shape) - 1 - axis_at))
    return gain


def rank_bounds(amount, lean):
    weights = [(1 << 20) // math.isqrt(grade ** lean) + 1 for grade in range(1, amount + 1)]
    deviation = 1 + sum(weights) // (1 << 30)
    return np.cumsum(np.array([max(1, weight // deviation) for weight in weights]))


def skewed_ids(stream_key, extent, count, slope):
    table = rank_bounds(count, slope)
    pick = jax.random.randint(jax.random.fold_in(stream_key, 1), extent, 0, int(table[count - 1]))
    rank = jnp.searchsorted(jnp.asarray(table, jnp.int32), pick, side="right")
    return jax.random.permutation(jax.random.fold_in(stream_key, 2), count)[rank].astype(jnp.int32)


def normal_values(own_key, shape, scale, reach, shards=(), held_as=jnp.bfloat16):
    loudness = shard_levels(own_key, shape, shards, -0.22, 0.18) if shards else 1.0
    result = jax.random.normal(own_key, shape, jnp.float32) * scale * loudness
    return jnp.minimum(jnp.maximum(result, -reach), reach).astype(held_as)


def setup_inputs(seed: int = 0) -> dict:
    keys = jax.random.split(jax.random.key(seed), 4)
    return {
        "integrals": draw_integrals(jax.random.fold_in(keys[3], 71), 0),
        "amplitudes": normal_values(keys[1], (PAIRS, OP), 1.0, 6.0, ((0, 8), (1, 4))),
        "labels": set_ends(skewed_ids(keys[2], (NT,), 8, 2), jax.random.fold_in(keys[2], 3), 0, 7).astype(jnp.int32),
    }


def reference(integrals, amplitudes, labels):
    def one_tile(index):
        slab_rows = lax.dynamic_slice_in_dim(integrals, index * TILE, TILE, 0)
        column_mask = jnp.repeat(labels == labels[index], TILE).astype(jnp.bfloat16)
        return jnp.dot(slab_rows * column_mask[None, :], amplitudes, preferred_element_type=jnp.float32)

    ladder = lax.map(one_tile, jnp.arange(NT, dtype=jnp.int32)).reshape(PAIRS, OP)
    mirrored = ladder.reshape(PAIRS, NOCC, NOCC).transpose(0, 2, 1).reshape(PAIRS, OP)
    return (0.5 * (ladder - mirrored)).astype(jnp.bfloat16)
```

```python
import functools
import math

import jax
import jax.numpy as jnp
from jax import lax
from jax.experimental import pallas as pl
from jax.experimental.pallas import tpu as pltpu
from jax.sharding import PartitionSpec as P

MESH = pl.DeviceIdType.MESH
UNROLL_UP_TO = 64


def repeat(low, high, body):
    if high - low <= UNROLL_UP_TO:
        for step in range(low, high):
            body(step)
    else:
        lax.fori_loop(low, high, lambda step, carry: (body(step), carry)[1], 0)


def kernel(tiles, owners, q, labels_hbm, integrals_hbm, amplitudes_hbm, out_ref,
           gathered, integrals, outgoing, wide, labels, load_sem, send_sem, recv_sem):
    cols, width = amplitudes_hbm.shape
    nocc = q * owners
    piece = q * q
    me, own = lax.axis_index("vir"), lax.axis_index("occ")

    def peer(step):
        return lax.rem(me + step // owners, tiles), lax.rem(own + step % owners, owners)

    barrier = pltpu.get_barrier_semaphore()

    def greet(step):
        pl.semaphore_signal(barrier, inc=1, device_id=peer(step), device_id_type=MESH)

    load_amplitudes = pltpu.make_async_copy(
        amplitudes_hbm, gathered.at[me, pl.ds(0, cols)], load_sem.at[0])
    load_integrals = pltpu.make_async_copy(integrals_hbm, integrals, load_sem.at[1])
    load_labels = pltpu.make_async_copy(labels_hbm, labels, load_sem.at[2])
    load_amplitudes.start()
    load_labels.start()
    load_integrals.start()
    repeat(1, tiles * owners, greet)

    load_amplitudes.wait()
    wide[pl.ds(0, cols)] = gathered[me, pl.ds(0, cols)].astype(jnp.float32)
    for owner in range(owners):
        rows = [wide[pl.ds(first * nocc + owner * q, q)] for first in range(q)]
        for first in range(q):
            wide[pl.ds(cols + owner * piece + first * q, q)] = rows[first]
    outgoing[...] = wide[pl.ds(cols, cols)].astype(jnp.bfloat16)
    gathered[me, pl.ds(cols + own * piece, piece)] = outgoing[pl.ds(own * piece, piece)]

    load_labels.wait()
    load_integrals.wait()

    def mask(tile):
        same = (labels[tile] == labels[me]).astype(jnp.float32)
        weight = jnp.full((width, width), same, jnp.float32).astype(jnp.bfloat16)
        rows = pl.ds(tile * width, width)
        integrals[rows] = integrals[rows] * weight

    repeat(0, tiles, mask)

    pl.semaphore_wait(barrier, tiles * owners - 1)

    def send(step):
        tile, owner = peer(step)
        shift = step // owners

        def share():
            pltpu.make_async_remote_copy(
                src_ref=outgoing.at[pl.ds(owner * piece, piece)],
                dst_ref=gathered.at[me, pl.ds(cols + own * piece, piece)],
                send_sem=send_sem.at[shift], recv_sem=recv_sem.at[me],
                device_id=(tile, owner), device_id_type=MESH).start()

        def block():
            pltpu.make_async_remote_copy(
                src_ref=gathered.at[me, pl.ds(0, cols)],
                dst_ref=gathered.at[me, pl.ds(0, cols)],
                send_sem=send_sem.at[shift], recv_sem=recv_sem.at[me],
                device_id=(tile, owner), device_id_type=MESH).start()
            pltpu.make_async_remote_copy(
                src_ref=outgoing.at[pl.ds(owner * piece, piece)],
                dst_ref=gathered.at[me, pl.ds(cols + own * piece, piece)],
                send_sem=send_sem.at[shift], recv_sem=recv_sem.at[me],
                device_id=(tile, owner), device_id_type=MESH).start()

        if isinstance(step, int):
            block() if step % owners == 0 else share()
        else:
            lax.cond(step % owners == 0, block, share)

    repeat(1, tiles * owners, send)

    def arrived(shift, rows, semaphores, index):
        held = gathered.at[0, pl.ds(0, rows)]
        pltpu.make_async_copy(held, held, semaphores.at[index]).wait()

    def product(tile):
        return jnp.dot(gathered[tile], integrals[pl.ds(pl.multiple_of(tile * width, width), width)],
                       preferred_element_type=jnp.float32)

    arrived(0, cols - piece, recv_sem, me)
    total = product(me)

    def add(shift, total):
        tile = lax.rem(me + shift, tiles)
        arrived(shift, 2 * cols, recv_sem, tile)
        return total + product(tile)

    if tiles <= UNROLL_UP_TO:
        for shift in range(1, tiles):
            total = add(shift, total)
    else:
        total = lax.fori_loop(1, tiles, add, total)

    wide[...] = total
    for first in range(q):
        ladder = wide[pl.ds(first * nocc, nocc)]
        mirrored = wide[pl.ds(cols + first, nocc, stride=q)]
        out_ref[pl.ds(first * nocc, nocc)] = (0.5 * (ladder - mirrored)).astype(jnp.bfloat16)

    arrived(0, cols - piece, send_sem, 0)
    repeat(1, tiles, lambda shift: arrived(shift, 2 * cols, send_sem, shift))


def per_device(integrals, amplitudes, labels):
    width, cols = amplitudes.shape
    tiles, owners = lax.axis_size("vir"), lax.axis_size("occ")
    q = math.isqrt(cols // owners)
    anywhere = pl.BlockSpec(memory_space=pltpu.HBM)
    flipped = pl.pallas_call(
        functools.partial(kernel, tiles, owners, q),
        out_shape=jax.ShapeDtypeStruct((cols, width), jnp.bfloat16),
        in_specs=[anywhere] * 3,
        out_specs=pl.BlockSpec(memory_space=pltpu.VMEM),
        scratch_shapes=[
            pltpu.VMEM((tiles, 2 * cols, width), jnp.bfloat16),
            pltpu.VMEM((tiles * width, width), jnp.bfloat16),
            pltpu.VMEM((cols, width), jnp.bfloat16),
            pltpu.VMEM((2 * cols, width), jnp.float32),
            pltpu.SMEM(labels.shape, jnp.int32),
            pltpu.SemaphoreType.DMA((3,)),
            pltpu.SemaphoreType.DMA((tiles,)),
            pltpu.SemaphoreType.DMA((tiles,)),
        ],
        compiler_params=pltpu.CompilerParams(
            collective_id=0, has_side_effects=True, vmem_limit_bytes=48 << 20),
        cost_estimate=pl.CostEstimate(
            flops=4 * tiles * width * width * cols,
            bytes_accessed=2 * tiles * width * (width + 2 * cols), transcendentals=0),
    )(labels, integrals, amplitudes.T)
    return flipped.T


def solution(mesh):
    placed = (P(None, "vir"), P("vir", "occ"), P())
    return jax.shard_map(
        per_device, mesh=mesh, in_specs=placed, out_specs=P("vir", "occ"), check_vma=False
    )
```

```python
import functools
import math

import jax
import jax.numpy as jnp
from jax import lax
from jax.experimental import pallas as pl
from jax.experimental.pallas import tpu as pltpu
from jax.sharding import PartitionSpec as P

MESH = pl.DeviceIdType.MESH
UNROLL_UP_TO = 64


def repeat(low, high, body):
    if high - low <= UNROLL_UP_TO:
        for step in range(low, high):
            body(step)
    else:
        lax.fori_loop(low, high, lambda step, carry: (body(step), carry)[1], 0)


def kernel(outer, inner, owners, q, labels_hbm, integrals_hbm, amplitudes_hbm, out_ref,
           gathered, integrals, wide, labels, load_sem, send_sem, first_sem, second_sem):
    cols, width = amplitudes_hbm.shape
    nocc, piece, tiles = q * owners, q * q, outer * inner
    me, own = lax.axis_index("vir"), lax.axis_index("occ")
    far, near = me // inner, lax.rem(me, inner)
    way = 1 - 2 * (far // max(outer // 2, 1))

    def line(step):
        return lax.rem(far + way * step + outer, outer) * inner + near

    def plane(step):
        return (far * inner + lax.rem(near + step // owners, inner),
                lax.rem(own + step % owners, owners))

    def held(tile, start, rows):
        return gathered.at[pl.ds(pl.multiple_of(tile * 2 * cols + start, piece), rows)]

    barrier = pltpu.get_barrier_semaphore()
    load_amplitudes = pltpu.make_async_copy(amplitudes_hbm, integrals.at[pl.ds(tiles * width, cols)],
                                            load_sem.at[0])
    load_integrals = pltpu.make_async_copy(integrals_hbm, integrals.at[pl.ds(0, tiles * width)],
                                           load_sem.at[1])
    load_labels = pltpu.make_async_copy(labels_hbm, labels, load_sem.at[2])
    load_amplitudes.start()
    load_labels.start()
    load_integrals.start()
    repeat(1, outer, lambda step: pl.semaphore_signal(
        barrier, inc=1, device_id=(line(step), own), device_id_type=MESH))
    repeat(1, inner * owners, lambda step: pl.semaphore_signal(
        barrier, inc=1, device_id=plane(step), device_id_type=MESH))

    load_amplitudes.wait()
    wide[pl.ds(0, cols)] = integrals[pl.ds(tiles * width, cols)].astype(jnp.float32)
    for owner in range(owners):
        for first in range(q):
            wide[pl.ds(cols + owner * piece + first * q, q)] = (
                wide[pl.ds(first * nocc + owner * q, q)])
    own_rows = pl.multiple_of(me * 2 * cols, piece)
    gathered[pl.ds(own_rows, cols)] = wide[pl.ds(cols, cols)].astype(jnp.bfloat16)

    def clear(tile):
        rows = pl.ds(pl.multiple_of(tile * 2 * cols + cols + own * piece, piece), piece)
        gathered[rows] = jnp.zeros((piece, width), jnp.bfloat16)

    repeat(0, tiles, clear)

    pl.semaphore_wait(barrier, outer + inner * owners - 2)

    def send_line(step):
        block = held(me, 0, cols)
        pltpu.make_async_remote_copy(
            src_ref=block, dst_ref=block, send_sem=send_sem.at[0], recv_sem=first_sem.at[me // inner],
            device_id=(line(step), own), device_id_type=MESH).start()

    repeat(1, outer, lambda step: send_line(outer - step))

    def send_plane(tile):
        block = held(tile, 0, cols)
        for step in range(1, inner * owners):
            to = plane(step)
            if step % owners:
                pltpu.make_async_remote_copy(
                    src_ref=held(tile, to[1] * piece, piece),
                    dst_ref=held(tile, cols + own * piece, piece),
                    send_sem=send_sem.at[0], recv_sem=second_sem.at[tile],
                    device_id=to, device_id_type=MESH).start()
            else:
                pltpu.make_async_remote_copy(
                    src_ref=block, dst_ref=block,
                    send_sem=send_sem.at[0], recv_sem=second_sem.at[tile],
                    device_id=to, device_id_type=MESH).start()

    def arrived(rows, semaphore):
        some = gathered.at[pl.ds(0, rows)]
        pltpu.make_async_copy(some, some, semaphore).wait()

    send_plane(me)

    load_labels.wait()
    load_integrals.wait()

    def mask(tile):
        same = (labels[tile] == labels[me]).astype(jnp.float32)
        weight = jnp.full((width, width), same, jnp.float32).astype(jnp.bfloat16)
        rows = pl.ds(tile * width, width)
        integrals[rows] = integrals[rows] * weight

    repeat(0, tiles, mask)

    def forward(step):
        tile = line(step)
        arrived(cols, first_sem.at[tile // inner])
        send_plane(tile)

    repeat(1, outer, forward)

    def add(step, total):
        tile = (line(step % outer) // inner) * inner + lax.rem(near + step // outer, inner)
        if isinstance(step, int):
            arrived(cols - piece if step < outer else 2 * cols - piece, second_sem.at[tile])
        else:
            lax.cond(step < outer, lambda: arrived(cols - piece, second_sem.at[tile]),
                     lambda: arrived(2 * cols - piece, second_sem.at[tile]))
        return total + jnp.dot(
            gathered[pl.ds(pl.multiple_of(tile * 2 * cols, piece), 2 * cols)],
            integrals[pl.ds(pl.multiple_of(tile * width, width), width)],
            preferred_element_type=jnp.float32)

    total = jnp.zeros((2 * cols, width), jnp.float32)
    if tiles <= UNROLL_UP_TO:
        for step in range(tiles):
            total = add(step, total)
    else:
        total = lax.fori_loop(0, tiles, add, total)

    wide[...] = total
    share = pl.multiple_of(own * piece, piece)
    wide[pl.ds(cols + share, piece)] = wide[pl.ds(share, piece)]
    for first in range(q):
        ladder = jnp.concatenate(
            [wide[pl.ds(owner * piece + first * q, q)] for owner in range(owners)], axis=0)
        mirrored = wide[pl.ds(cols + first, nocc, stride=q)]
        out_ref[pl.ds(first * nocc, nocc)] = (0.5 * (ladder - mirrored)).astype(jnp.bfloat16)

    arrived((outer - 1) * cols + outer * ((inner - 1) * cols + inner * (cols - piece)),
            send_sem.at[0])


def per_device(integrals, amplitudes, labels):
    width, cols = amplitudes.shape
    tiles, owners = lax.axis_size("vir"), lax.axis_size("occ")
    q = math.isqrt(cols // owners)
    inner = 1 if tiles % 2 else 2
    outer = tiles // inner
    anywhere = pl.BlockSpec(memory_space=pltpu.HBM)
    flipped = pl.pallas_call(
        functools.partial(kernel, outer, inner, owners, q),
        out_shape=jax.ShapeDtypeStruct((cols, width), jnp.bfloat16),
        in_specs=[anywhere] * 3,
        out_specs=pl.BlockSpec(memory_space=pltpu.VMEM),
        scratch_shapes=[
            pltpu.VMEM((tiles * 2 * cols, width), jnp.bfloat16),
            pltpu.VMEM((tiles * width + cols, width), jnp.bfloat16),
            pltpu.VMEM((2 * cols, width), jnp.float32),
            pltpu.SMEM(labels.shape, jnp.int32),
            pltpu.SemaphoreType.DMA((3,)),
            pltpu.SemaphoreType.DMA((1,)),
            pltpu.SemaphoreType.DMA((outer,)),
            pltpu.SemaphoreType.DMA((tiles,)),
        ],
        compiler_params=pltpu.CompilerParams(
            collective_id=0, has_side_effects=True, vmem_limit_bytes=62 << 20),
        cost_estimate=pl.CostEstimate(
            flops=4 * tiles * width * width * cols,
            bytes_accessed=2 * tiles * width * (width + 2 * cols), transcendentals=0),
    )(labels, integrals, amplitudes.T)
    return flipped.T


def solution(mesh):
    placed = (P(None, "vir"), P("vir", "occ"), P())
    return jax.shard_map(
        per_device, mesh=mesh, in_specs=placed, out_specs=P("vir", "occ"), check_vma=False
    )
```

```python
import functools
import math

import jax
import jax.numpy as jnp
from jax import lax
from jax.experimental import pallas as pl
from jax.experimental.pallas import tpu as pltpu
from jax.sharding import PartitionSpec as P

MESH = pl.DeviceIdType.MESH
UNROLL_UP_TO = 64


def repeat(low, high, body):
    if high - low <= UNROLL_UP_TO:
        for step in range(low, high):
            body(step)
    else:
        lax.fori_loop(low, high, lambda step, carry: (body(step), carry)[1], 0)


def kernel(outer, inner, owners, q, labels_hbm, integrals_hbm, amplitudes_hbm, out_ref,
           gathered, integrals, wide, labels, load_sem, send_sem, recv_sem):
    cols, width = amplitudes_hbm.shape
    nocc, piece, tiles = q * owners, q * q, outer * inner
    me, own = lax.axis_index("vir"), lax.axis_index("occ")
    far, near = me // inner, lax.rem(me, inner)
    way = 1 - 2 * (far // max(outer // 2, 1))

    def peer(step):
        return (lax.rem(far + way * (step // (inner * owners)) + outer, outer) * inner
                + lax.rem(near + step // owners % inner, inner),
                lax.rem(own + step % owners, owners))

    def held(tile, start, rows):
        return gathered.at[pl.ds(pl.multiple_of(tile * 2 * cols + start, piece), rows)]

    barrier = pltpu.get_barrier_semaphore()
    load_amplitudes = pltpu.make_async_copy(amplitudes_hbm, integrals.at[pl.ds(tiles * width, cols)],
                                            load_sem.at[0])
    load_integrals = pltpu.make_async_copy(integrals_hbm, integrals.at[pl.ds(0, tiles * width)],
                                           load_sem.at[1])
    load_labels = pltpu.make_async_copy(labels_hbm, labels, load_sem.at[2])
    load_amplitudes.start()
    load_labels.start()
    load_integrals.start()
    repeat(1, tiles * owners, lambda step: pl.semaphore_signal(
        barrier, inc=1, device_id=peer(step), device_id_type=MESH))

    load_amplitudes.wait()
    wide[pl.ds(0, cols)] = integrals[pl.ds(tiles * width, cols)].astype(jnp.float32)
    for owner in range(owners):
        for first in range(q):
            wide[pl.ds(cols + owner * piece + first * q, q)] = (
                wide[pl.ds(first * nocc + owner * q, q)])
    own_rows = pl.multiple_of(me * 2 * cols, piece)
    gathered[pl.ds(own_rows, cols)] = wide[pl.ds(cols, cols)].astype(jnp.bfloat16)

    def clear(tile):
        rows = pl.ds(pl.multiple_of(tile * 2 * cols + cols + own * piece, piece), piece)
        gathered[rows] = jnp.zeros((piece, width), jnp.bfloat16)

    repeat(0, tiles, clear)

    pl.semaphore_wait(barrier, tiles * owners - 1)

    def send(tile):
        def copy(source, target, owner):
            pltpu.make_async_remote_copy(
                src_ref=source, dst_ref=target, send_sem=send_sem.at[0],
                recv_sem=recv_sem.at[me], device_id=(tile, owner), device_id_type=MESH).start()

        @pl.when(tile != me)
        def _():
            copy(held(me, 0, cols), held(me, 0, cols), own)

        for step in range(1, owners):
            owner = lax.rem(own + step, owners)
            copy(held(me, owner * piece, piece), held(me, cols + own * piece, piece), owner)

    repeat(0, tiles, send)

    def arrived(rows, semaphore):
        some = gathered.at[pl.ds(0, rows)]
        pltpu.make_async_copy(some, some, semaphore).wait()

    load_labels.wait()
    load_integrals.wait()

    def mask(tile):
        same = (labels[tile] == labels[me]).astype(jnp.float32)
        weight = jnp.full((width, width), same, jnp.float32).astype(jnp.bfloat16)
        rows = pl.ds(tile * width, width)
        integrals[rows] = integrals[rows] * weight

    repeat(0, tiles, mask)

    def add(step, total):
        tile = peer(step * owners)[0]
        arrived(cols - piece if isinstance(step, int) and step == 0 else 2 * cols - piece,
                recv_sem.at[tile])
        return total + jnp.dot(
            gathered[pl.ds(pl.multiple_of(tile * 2 * cols, piece), 2 * cols)],
            integrals[pl.ds(pl.multiple_of(tile * width, width), width)],
            preferred_element_type=jnp.float32)

    total = add(0, jnp.zeros((2 * cols, width), jnp.float32))
    if tiles <= UNROLL_UP_TO:
        for step in range(1, tiles):
            total = add(step, total)
    else:
        total = lax.fori_loop(1, tiles, add, total)

    wide[...] = total
    share = pl.multiple_of(own * piece, piece)
    wide[pl.ds(cols + share, piece)] = wide[pl.ds(share, piece)]
    for first in range(q):
        ladder = jnp.concatenate(
            [wide[pl.ds(owner * piece + first * q, q)] for owner in range(owners)], axis=0)
        mirrored = wide[pl.ds(cols + first, nocc, stride=q)]
        out_ref[pl.ds(first * nocc, nocc)] = (0.5 * (ladder - mirrored)).astype(jnp.bfloat16)

    arrived((tiles - 1) * cols + tiles * (cols - piece), send_sem.at[0])


def per_device(integrals, amplitudes, labels):
    width, cols = amplitudes.shape
    tiles, owners = lax.axis_size("vir"), lax.axis_size("occ")
    q = math.isqrt(cols // owners)
    inner = 1 if tiles % 2 else 2
    outer = tiles // inner
    anywhere = pl.BlockSpec(memory_space=pltpu.HBM)
    flipped = pl.pallas_call(
        functools.partial(kernel, outer, inner, owners, q),
        out_shape=jax.ShapeDtypeStruct((cols, width), jnp.bfloat16),
        in_specs=[anywhere] * 3,
        out_specs=pl.BlockSpec(memory_space=pltpu.VMEM),
        scratch_shapes=[
            pltpu.VMEM((tiles * 2 * cols, width), jnp.bfloat16),
            pltpu.VMEM((tiles * width + cols, width), jnp.bfloat16),
            pltpu.VMEM((2 * cols, width), jnp.float32),
            pltpu.SMEM(labels.shape, jnp.int32),
            pltpu.SemaphoreType.DMA((3,)),
            pltpu.SemaphoreType.DMA((1,)),
            pltpu.SemaphoreType.DMA((tiles,)),
        ],
        compiler_params=pltpu.CompilerParams(
            collective_id=0, has_side_effects=True, vmem_limit_bytes=32 << 20),
        cost_estimate=pl.CostEstimate(
            flops=4 * tiles * width * width * cols,
            bytes_accessed=2 * tiles * width * (width + 2 * cols), transcendentals=0),
    )(*(pltpu.with_memory_space_constraint(a, pltpu.HBM) for a in (labels, integrals, amplitudes.T)))
    return flipped.T


def solution(mesh):
    placed = (P(None, "vir"), P("vir", "occ"), P())
    return jax.shard_map(
        per_device, mesh=mesh, in_specs=placed, out_specs=P("vir", "occ"), check_vma=False
    )
```

```python
import functools
import math

import jax
import jax.numpy as jnp
from jax import lax
from jax.experimental import pallas as pl
from jax.experimental.pallas import tpu as pltpu
from jax.sharding import PartitionSpec as P

MESH = pl.DeviceIdType.MESH
UNROLL_UP_TO = 64


def repeat(low, high, body):
    if high - low <= UNROLL_UP_TO:
        for step in range(low, high):
            body(step)
    else:
        lax.fori_loop(low, high, lambda step, carry: (body(step), carry)[1], 0)


def kernel(outer, inner, owners, q, labels_hbm, integrals_hbm, amplitudes_hbm, out_ref,
           gathered, integrals, wide, labels, load_sem, send_sem, recv_sem):
    cols, width = amplitudes_hbm.shape
    nocc, piece, tiles = q * owners, q * q, outer * inner
    me, own = lax.axis_index("vir"), lax.axis_index("occ")
    far, near = me // inner, lax.rem(me, inner)
    way = 1 - 2 * (far // max(outer // 2, 1))

    def peer(step):
        return (lax.rem(far + way * (step // (inner * owners)) + outer, outer) * inner
                + lax.rem(near + step // owners % inner, inner),
                lax.rem(own + step % owners, owners))

    def held(tile, start, rows):
        return gathered.at[pl.ds(pl.multiple_of(tile * 2 * cols + start, piece), rows)]

    barrier = pltpu.get_barrier_semaphore()
    load_amplitudes = pltpu.make_async_copy(amplitudes_hbm, integrals.at[pl.ds(tiles * width, cols)],
                                            load_sem.at[0])
    load_integrals = pltpu.make_async_copy(integrals_hbm, integrals.at[pl.ds(0, tiles * width)],
                                           load_sem.at[1])
    load_labels = pltpu.make_async_copy(labels_hbm, labels, load_sem.at[2])
    load_amplitudes.start()
    load_labels.start()
    load_integrals.start()
    repeat(1, tiles * owners, lambda step: pl.semaphore_signal(
        barrier, inc=1, device_id=peer(step), device_id_type=MESH))

    load_amplitudes.wait()
    wide[pl.ds(0, cols)] = integrals[pl.ds(tiles * width, cols)].astype(jnp.float32)
    for owner in range(owners):
        for first in range(q):
            wide[pl.ds(cols + owner * piece + first * q, q)] = (
                wide[pl.ds(first * nocc + owner * q, q)])
    own_rows = pl.multiple_of(me * 2 * cols, piece)
    gathered[pl.ds(own_rows, cols)] = wide[pl.ds(cols, cols)].astype(jnp.bfloat16)

    def clear(tile):
        rows = pl.ds(pl.multiple_of(tile * 2 * cols + cols + own * piece, piece), piece)
        gathered[rows] = jnp.zeros((piece, width), jnp.bfloat16)

    repeat(0, tiles, clear)

    pl.semaphore_wait(barrier, tiles * owners - 1)

    def send(tile):
        def copy(source, target, owner):
            pltpu.make_async_remote_copy(
                src_ref=source, dst_ref=target, send_sem=send_sem.at[0],
                recv_sem=recv_sem.at[me], device_id=(tile, owner), device_id_type=MESH).start()

        for owner in range(owners):
            @pl.when((owner == own) & (tile != me))
            def _():
                copy(held(me, 0, cols), held(me, 0, cols), owner)

            @pl.when(owner != own)
            def _():
                copy(held(me, owner * piece, piece), held(me, cols + own * piece, piece), owner)

    repeat(0, tiles, send)

    def arrived(rows, semaphore):
        some = gathered.at[pl.ds(0, rows)]
        pltpu.make_async_copy(some, some, semaphore).wait()

    load_labels.wait()
    load_integrals.wait()

    def mask(tile):
        same = (labels[tile] == labels[me]).astype(jnp.float32)
        weight = jnp.full((width, width), same, jnp.float32).astype(jnp.bfloat16)
        rows = pl.ds(tile * width, width)
        integrals[rows] = integrals[rows] * weight

    repeat(0, tiles, mask)

    def add(step, total):
        tile = peer(step * owners)[0]
        arrived(cols - piece if isinstance(step, int) and step == 0 else 2 * cols - piece,
                recv_sem.at[tile])
        return total + jnp.dot(
            gathered[pl.ds(pl.multiple_of(tile * 2 * cols, piece), 2 * cols)],
            integrals[pl.ds(pl.multiple_of(tile * width, width), width)],
            preferred_element_type=jnp.float32)

    total = add(0, jnp.zeros((2 * cols, width), jnp.float32))
    if tiles <= UNROLL_UP_TO:
        for step in range(1, tiles):
            total = add(step, total)
    else:
        total = lax.fori_loop(1, tiles, add, total)

    wide[...] = total
    share = pl.multiple_of(own * piece, piece)
    wide[pl.ds(cols + share, piece)] = wide[pl.ds(share, piece)]
    for first in range(q):
        ladder = jnp.concatenate(
            [wide[pl.ds(owner * piece + first * q, q)] for owner in range(owners)], axis=0)
        mirrored = wide[pl.ds(cols + first, nocc, stride=q)]
        out_ref[pl.ds(first * nocc, nocc)] = (0.5 * (ladder - mirrored)).astype(jnp.bfloat16)

    arrived((tiles - 1) * cols + tiles * (cols - piece), send_sem.at[0])


def per_device(integrals, amplitudes, labels):
    width, cols = amplitudes.shape
    tiles, owners = lax.axis_size("vir"), lax.axis_size("occ")
    q = math.isqrt(cols // owners)
    inner = 1 if tiles % 2 else 2
    outer = tiles // inner
    anywhere = pl.BlockSpec(memory_space=pltpu.HBM)
    flipped = pl.pallas_call(
        functools.partial(kernel, outer, inner, owners, q),
        out_shape=jax.ShapeDtypeStruct((cols, width), jnp.bfloat16),
        in_specs=[anywhere] * 3,
        out_specs=pl.BlockSpec(memory_space=pltpu.VMEM),
        scratch_shapes=[
            pltpu.VMEM((tiles * 2 * cols, width), jnp.bfloat16),
            pltpu.VMEM((tiles * width + cols, width), jnp.bfloat16),
            pltpu.VMEM((2 * cols, width), jnp.float32),
            pltpu.SMEM(labels.shape, jnp.int32),
            pltpu.SemaphoreType.DMA((3,)),
            pltpu.SemaphoreType.DMA((1,)),
            pltpu.SemaphoreType.DMA((tiles,)),
        ],
        compiler_params=pltpu.CompilerParams(
            collective_id=0, has_side_effects=True, vmem_limit_bytes=32 << 20),
        cost_estimate=pl.CostEstimate(
            flops=4 * tiles * width * width * cols,
            bytes_accessed=2 * tiles * width * (width + 2 * cols), transcendentals=0),
    )(*(pltpu.with_memory_space_constraint(a, pltpu.HBM) for a in (labels, integrals, amplitudes.T)))
    return flipped.T


def solution(mesh):
    placed = (P(None, "vir"), P("vir", "occ"), P())
    return jax.shard_map(
        per_device, mesh=mesh, in_specs=placed, out_specs=P("vir", "occ"), check_vma=False
    )
```

```python
import functools
import math

import jax
import jax.numpy as jnp
from jax import lax
from jax.experimental import pallas as pl
from jax.experimental.pallas import tpu as pltpu
from jax.sharding import PartitionSpec as P

MESH = pl.DeviceIdType.MESH
UNROLL_UP_TO = 64


def repeat(low, high, body):
    if high - low <= UNROLL_UP_TO:
        for step in range(low, high):
            body(step)
    else:
        lax.fori_loop(low, high, lambda step, carry: (body(step), carry)[1], 0)


def kernel(outer, inner, owners, q, labels_hbm, integrals_hbm, amplitudes_hbm, out_ref,
           gathered, integrals, wide, labels, load_sem, send_sem, recv_sem):
    cols, width = amplitudes_hbm.shape
    nocc, piece, tiles = q * owners, q * q, outer * inner
    me, own = lax.axis_index("vir"), lax.axis_index("occ")
    far, near = me // inner, lax.rem(me, inner)
    way = 1 - 2 * (far // max(outer // 2, 1))

    def peer(step):
        return (lax.rem(far + way * (step // (inner * owners)) + outer, outer) * inner
                + lax.rem(near + step // owners % inner, inner),
                lax.rem(own + step % owners, owners))

    def held(tile, start, rows):
        return gathered.at[pl.ds(pl.multiple_of(tile * 2 * cols + start, piece), rows)]

    barrier = pltpu.get_barrier_semaphore()
    load_amplitudes = pltpu.make_async_copy(amplitudes_hbm, integrals.at[pl.ds(tiles * width, cols)],
                                            load_sem.at[0])
    load_integrals = pltpu.make_async_copy(integrals_hbm, integrals.at[pl.ds(0, tiles * width)],
                                           load_sem.at[1])
    load_labels = pltpu.make_async_copy(labels_hbm, labels, load_sem.at[2])
    load_amplitudes.start()
    load_labels.start()
    load_integrals.start()
    repeat(1, tiles * owners, lambda step: pl.semaphore_signal(
        barrier, inc=1, device_id=peer(tiles * owners - step), device_id_type=MESH))

    load_amplitudes.wait()
    wide[pl.ds(0, cols)] = integrals[pl.ds(tiles * width, cols)].astype(jnp.float32)
    for owner in range(owners):
        for first in range(q):
            wide[pl.ds(cols + owner * piece + first * q, q)] = (
                wide[pl.ds(first * nocc + owner * q, q)])
    own_rows = pl.multiple_of(me * 2 * cols, piece)
    gathered[pl.ds(own_rows, cols)] = wide[pl.ds(cols, cols)].astype(jnp.bfloat16)

    def clear(tile):
        rows = pl.ds(pl.multiple_of(tile * 2 * cols + cols + own * piece, piece), piece)
        gathered[rows] = jnp.zeros((piece, width), jnp.bfloat16)

    repeat(0, tiles, clear)

    pl.semaphore_wait(barrier, tiles * owners - 1)

    def send(tile):
        def copy(source, target, owner):
            pltpu.make_async_remote_copy(
                src_ref=source, dst_ref=target, send_sem=send_sem.at[0],
                recv_sem=recv_sem.at[me], device_id=(tile, owner), device_id_type=MESH).start()

        for owner in range(owners):
            @pl.when((owner == own) & (tile != me))
            def _():
                copy(held(me, 0, cols), held(me, 0, cols), owner)

            @pl.when(owner != own)
            def _():
                copy(held(me, owner * piece, piece), held(me, cols + own * piece, piece), owner)

    repeat(0, tiles, send)

    def arrived(rows, semaphore):
        some = gathered.at[pl.ds(0, rows)]
        pltpu.make_async_copy(some, some, semaphore).wait()

    load_labels.wait()
    load_integrals.wait()

    def mask(tile):
        same = (labels[tile] == labels[me]).astype(jnp.float32)
        weight = jnp.full((width, width), same, jnp.float32).astype(jnp.bfloat16)
        rows = pl.ds(tile * width, width)
        integrals[rows] = integrals[rows] * weight

    repeat(0, tiles, mask)

    def add(step, total):
        tile = peer(step * owners)[0]
        arrived(cols - piece if isinstance(step, int) and step == 0 else 2 * cols - piece,
                recv_sem.at[tile])
        return total + jnp.dot(
            gathered[pl.ds(pl.multiple_of(tile * 2 * cols, piece), 2 * cols)],
            integrals[pl.ds(pl.multiple_of(tile * width, width), width)],
            preferred_element_type=jnp.float32)

    total = add(0, jnp.zeros((2 * cols, width), jnp.float32))
    if tiles <= UNROLL_UP_TO:
        for step in range(1, tiles):
            total = add(step, total)
    else:
        total = lax.fori_loop(1, tiles, add, total)

    wide[...] = total
    share = pl.multiple_of(own * piece, piece)
    wide[pl.ds(cols + share, piece)] = wide[pl.ds(share, piece)]
    for first in range(q):
        ladder = jnp.concatenate(
            [wide[pl.ds(owner * piece + first * q, q)] for owner in range(owners)], axis=0)
        mirrored = wide[pl.ds(cols + first, nocc, stride=q)]
        out_ref[pl.ds(first * nocc, nocc)] = (0.5 * (ladder - mirrored)).astype(jnp.bfloat16)

    arrived((tiles - 1) * cols + tiles * (cols - piece), send_sem.at[0])


def per_device(integrals, amplitudes, labels):
    width, cols = amplitudes.shape
    tiles, owners = lax.axis_size("vir"), lax.axis_size("occ")
    q = math.isqrt(cols // owners)
    inner = 1 if tiles % 2 else 2
    outer = tiles // inner
    anywhere = pl.BlockSpec(memory_space=pltpu.HBM)
    flipped = pl.pallas_call(
        functools.partial(kernel, outer, inner, owners, q),
        out_shape=jax.ShapeDtypeStruct((cols, width), jnp.bfloat16),
        in_specs=[anywhere] * 3,
        out_specs=pl.BlockSpec(memory_space=pltpu.VMEM),
        scratch_shapes=[
            pltpu.VMEM((tiles * 2 * cols, width), jnp.bfloat16),
            pltpu.VMEM((tiles * width + cols, width), jnp.bfloat16),
            pltpu.VMEM((2 * cols, width), jnp.float32),
            pltpu.SMEM(labels.shape, jnp.int32),
            pltpu.SemaphoreType.DMA((3,)),
            pltpu.SemaphoreType.DMA((1,)),
            pltpu.SemaphoreType.DMA((tiles,)),
        ],
        compiler_params=pltpu.CompilerParams(
            collective_id=0, has_side_effects=True, vmem_limit_bytes=32 << 20),
        cost_estimate=pl.CostEstimate(
            flops=4 * tiles * width * width * cols,
            bytes_accessed=2 * tiles * width * (width + 2 * cols), transcendentals=0),
    )(*(pltpu.with_memory_space_constraint(a, pltpu.HBM) for a in (labels, integrals, amplitudes.T)))
    return flipped.T


def solution(mesh):
    placed = (P(None, "vir"), P("vir", "occ"), P())
    return jax.shard_map(
        per_device, mesh=mesh, in_specs=placed, out_specs=P("vir", "occ"), check_vma=False
    )
```
